768 devices in a mesh: row: 48 (over z, x_hi, core), col: 16 (over y, x_lo).
Axes of the slice: x: 4 (x_hi: 2, x_lo: 2; x = x_hi * 2 + x_lo), y: 8, z: 12, core: 2. Of those that a mesh axis runs over, the one named last changes fastest.
Arguments:
- vectors: bfloat16 [8, 196608], P(None, ('row', 'col')), may hold values from -6 to 6
- blocks: bfloat16 [48, 16, 32, 128, 128], P('row', 'col'), may hold values from -0.0625 to 0.0625
- row_index: int32 [48, 16, 32], P('row', 'col'), may hold values from 0 to 31, as said below
- col_index: int32 [48, 16, 32], P('row', 'col'), may hold values from 0 to 95
- live: int32 [48, 16], P('row', 'col'), may hold values from 1 to 32, as said below
Outputs:
- applied: float32 [8, 196608], P(None, ('row', 'col'))
The draws below stay inside these ranges and needn't reach their ends.
Inputs may be any that keep to these rules, and one draw needn't show every extreme that they name: row_index lies in 0 to 31 and col_index in 0 to 95; live slots are the first live[i, j] of their cell, each lies on or above the block diagonal, and no pair repeats within a cell. Some cell holds 32 live slots in every draw.
All inputs are finite; a program needn't handle non-finite values.
Results may differ from the reference program's by a relative error of at most 0.0003.
Values may be sent and summed in bfloat16 or wider, within the bound.
A program may use at most 32 MiB of HBM per device.

```python
import jax
import jax.numpy as jnp
from jax import lax

BS = 128
NVEC = 8
PB = 2
SLOTS = 32
N = 196608
N_ROW = 48
N_COL = 16


def table_draw(key):
    row_blocks = N_COL * PB
    col_blocks = N_ROW * PB
    pairs = row_blocks * col_blocks
    cells = N_ROW * N_COL
    local_a = jnp.arange(pairs, dtype=jnp.int32) // col_blocks
    local_b = jnp.arange(pairs, dtype=jnp.int32) % col_blocks
    wanted = jax.random.randint(jax.random.fold_in(key, 7001), (cells,), SLOTS // 2 + 1, SLOTS + 1).astype(jnp.int32)
    full_cell = jax.random.randint(jax.random.fold_in(key, 7002), (), 0, N_COL).astype(jnp.int32)
    wanted = jnp.where(jnp.arange(cells, dtype=jnp.int32) == full_cell, SLOTS, wanted).astype(jnp.int32)

    def one_cell(device, target):
        grid_row = device // N_COL
        grid_col = device % N_COL
        grow = (grid_row * N_COL + local_a // PB) * PB + local_a % PB
        gcol = (local_b // PB * N_COL + grid_col) * PB + local_b % PB
        usable = grow <= gcol
        order = jax.random.permutation(jax.random.fold_in(key, device), pairs).astype(jnp.int32)
        priority = jnp.where(usable, order, order + pairs)
        picked = jnp.argsort(priority, stable=True)[:SLOTS]
        count = jnp.minimum(target, jnp.sum(usable.astype(jnp.int32)))
        return (local_a[picked], local_b[picked], count)
    firsts, seconds, counts = jax.vmap(one_cell)(jnp.arange(cells, dtype=jnp.int32), wanted)
    return (firsts.reshape(N_ROW, N_COL, SLOTS).astype(jnp.int32), seconds.reshape(N_ROW, N_COL, SLOTS).astype(jnp.int32), counts.reshape(N_ROW, N_COL).astype(jnp.int32))


def draw_row_index(key, part):
    return table_draw(key)[0]


def draw_col_index(key, part):
    return table_draw(key)[1]


def draw_live(key, part):
    return table_draw(key)[2]


def block_scale(rng, shape, cuts, smallest, high):
    loudness = 1.0
    for position, shards_of in cuts:
        draws = jax.random.uniform(jax.random.fold_in(jax.random.fold_in(rng, 6), position), (shards_of,), jnp.float32, smallest / len(cuts), high / len(cuts))
        loudness = loudness * jnp.repeat(jnp.exp(draws), shape[position] // shards_of).reshape((-1,) + (1,) * (len(shape) - 1 - position))
    return loudness


def bell_draw(stream_key, dims, deviation, reach, shards=(), kind=jnp.bfloat16):
    drawn = deviation * jax.random.normal(stream_key, dims, jnp.float32)
    if shards:
        drawn = drawn * block_scale(stream_key, dims, shards, -0.22, 0.18)
    return jnp.clip(drawn, -reach, reach).astype(kind)


def setup_inputs(seed: int = 0) -> dict:
    splits = jax.random.split(jax.random.key(seed), 6)
    return {
        "vectors": bell_draw(splits[0], (NVEC, N), 1.0, 6.0, ((1, 768),)),
        "blocks": bell_draw(splits[1], (N_ROW, N_COL, SLOTS, BS, BS), (BS * 64) ** -0.5, 0.0625, ((0, 48), (1, 16))),
        "row_index": draw_row_index(jax.random.fold_in(splits[5], 71), 0),
        "col_index": draw_col_index(jax.random.fold_in(splits[5], 71), 0),
        "live": draw_live(jax.random.fold_in(splits[5], 71), 0),
    }


def global_rows(row_index, col_index):
    grid_row = jnp.arange(N_ROW, dtype=jnp.int32)[:, None, None]
    grid_col = jnp.arange(N_COL, dtype=jnp.int32)[None, :, None]
    grow = (grid_row * N_COL + row_index // PB) * PB + row_index % PB
    gcol = ((col_index // PB) * N_COL + grid_col) * PB + col_index % PB
    return grow.astype(jnp.int32), gcol.astype(jnp.int32)


def reference(vectors, blocks, row_index, col_index, live):
    grow, gcol = global_rows(row_index, col_index)
    slot_ids = jnp.arange(SLOTS, dtype=jnp.int32)[None, None, :]
    weight = (slot_ids < live[:, :, None]).astype(jnp.float32)
    nblk = N // BS
    states = vectors.astype(jnp.float32).reshape(NVEC, nblk, BS)

    def per_row(total, index):
        block_row = blocks[index].astype(jnp.float32)
        rows_here = grow[index]
        cols_here = gcol[index]
        mask = weight[index]
        from_cols = states[:, cols_here]
        from_rows = states[:, rows_here]
        upper = jnp.einsum("ckij,vckj->vcki", block_row, from_cols) * mask[None, :, :, None]
        lower = jnp.einsum("ckij,vcki->vckj", block_row, from_rows) * mask[None, :, :, None]
        total = total.at[:, rows_here].add(upper)
        total = total.at[:, cols_here].add(lower)
        return total, None

    start = jnp.zeros((NVEC, nblk, BS), jnp.float32)
    total, _ = lax.scan(per_row, start, jnp.arange(N_ROW, dtype=jnp.int32))
    return total.reshape(NVEC, N)
```

```python
import functools

import jax
import jax.numpy as jnp
from jax import lax
from jax.experimental import pallas as pl
from jax.experimental.pallas import tpu as pltpu
from jax.sharding import PartitionSpec as P

MESH = pl.DeviceIdType.MESH
BF16 = jnp.bfloat16
F32 = jnp.float32


def iota(shape, dim):
    return lax.broadcasted_iota(jnp.int32, shape, dim)


def split_dot(one_hot, terms):
    high = terms.astype(BF16)
    low = (terms - high.astype(F32)).astype(BF16)
    return jnp.dot(one_hot, high, preferred_element_type=F32) + jnp.dot(one_hot, low, preferred_element_type=F32)


def loop(first, last, body):
    def step(index, carry):
        body(index)
        return carry

    lax.fori_loop(first, last, step, 0)


def kernel(
    n_chip, n_col, vec_hbm, blocks, row_hbm, col_hbm, live_hbm, out,
    vec, row_index, col_index, live, held, row_st, col_st, row_pick, col_pick, row_place, col_place,
    picked, terms, low, low_sib, low_in, up, up_in,
    fetch_sem, row_send, row_recv, col_send, col_recv, low_send, low_recv, up_send, up_recv, sib_send, sib_recv,
    sib_ready,
):
    slots, width = held.shape[0], held.shape[1]
    nvec = vec.shape[0]
    piece = 2 * nvec
    rows = slots * nvec
    n_y = n_col // 2
    row, col = lax.axis_index("row"), lax.axis_index("col")
    chip, core = row // 2, row % 2
    sibling = {"row": row + 1 - 2 * core, "col": col}

    turn = jnp.where(row == 0, 1, 0)

    def col_of(rank):
        place = (rank + turn) % n_col
        key = place // 2
        y = jnp.where(key % 2 == 0, key // 2, n_y - (key + 1) // 2)
        return y * 2 + place % 2

    y = col // 2
    key = jnp.where(2 * y < n_y + n_y % 2, 2 * y, 2 * (n_y - y) - 1)
    rank = (key * 2 + col % 2 - turn + n_col) % n_col

    fetches = [
        pltpu.make_async_copy(source, target, fetch_sem.at[index])
        for index, (source, target) in enumerate(
            ((vec_hbm, vec), (row_hbm, row_index), (col_hbm, col_index), (live_hbm, live), (blocks.at[0, 0], held))
        )
    ]
    for fetch in fetches:
        fetch.start()

    def pieces(slot):
        return pl.ds(pl.multiple_of(slot * piece, piece), piece)

    col_st[...] = jnp.zeros_like(col_st)
    mine = core * n_chip + chip

    barrier = pltpu.get_barrier_semaphore()

    def greet(device):
        pl.semaphore_signal(barrier, inc=1, device_id=device, device_id_type=MESH)

    loop(rank + 1, n_col, lambda r: greet({"row": row, "col": col_of(r)}))
    loop(chip + 1, n_chip, lambda q: greet({"row": q * 2 + core, "col": col}))

    @pl.when(core == 1)
    def _():
        greet(sibling)

    fetches[0].wait()
    own = vec[...].astype(F32)
    own = jnp.concatenate([own[:, :width], own[:, width:]], axis=0).astype(BF16)
    col_st[pieces(mine)] = own
    row_st[pieces(col)] = own

    earlier = rank + chip + 1 - core

    @pl.when(earlier > 0)
    def _():
        pl.semaphore_wait(barrier, earlier)

    @pl.when(core == 0)
    def _():
        pl.semaphore_signal(sib_ready, inc=1, device_id=sibling, device_id_type=MESH)

    def col_copy(source, target):
        place = pieces(core * n_chip + source)
        return pltpu.make_async_remote_copy(
            col_st.at[place], col_st.at[place], col_send.at[target], col_recv.at[source],
            device_id={"row": target * 2 + core, "col": col}, device_id_type=MESH,
        )

    def row_copy(source, target):
        return pltpu.make_async_remote_copy(
            row_st.at[pieces(source)], row_st.at[pieces(source)], row_send.at[target], row_recv.at[source],
            device_id={"row": row, "col": target}, device_id_type=MESH,
        )

    loop(0, chip, lambda q: col_copy(chip, q).start())
    loop(0, rank, lambda r: row_copy(col, col_of(r)).start())

    for fetch in fetches[1:4]:
        fetch.wait()
    alive = iota((1, slots), 1) < live[...]
    row_ids = jnp.where(alive, row_index[0], -1).astype(F32)
    col_ids = jnp.where(alive, col_index[0], -1).astype(F32)
    spread = (iota((slots, rows), 1) // nvec == iota((slots, rows), 0)).astype(F32).astype(BF16)
    spread_t = (iota((rows, slots), 0) // nvec == iota((rows, slots), 1)).astype(F32)

    def row_target(ids, vector):
        return jnp.where(ids < 0, -1, ids * nvec + vector)

    def col_target(ids, vector):
        place = (ids // 2) % 2 * n_chip + ids // 4
        return jnp.where(ids < 0, -1, place * piece + ids % 2 * nvec + vector)

    for ids, target, pick, place in (
        (row_ids, row_target, row_pick, row_place),
        (col_ids, col_target, col_pick, col_place),
    ):
        count = place.shape[0]
        lane = jnp.dot(ids.astype(BF16), spread, preferred_element_type=F32).astype(jnp.int32)
        lane = target(lane, iota((1, rows), 1) % nvec)
        place[...] = (iota((count, rows), 0) == lane).astype(F32).astype(BF16)
        line = jnp.sum(spread_t * ids, axis=1, keepdims=True).astype(jnp.int32)
        line = target(line, iota((rows, 1), 0) % nvec)
        pick[...] = (iota((rows, count), 1) == line).astype(F32).astype(BF16)

    def answer(r):
        other = col_of(r)
        row_copy(other, col).wait_recv()
        row_copy(col, other).start()

    loop(rank + 1, n_col, answer)
    loop(0, rank, lambda r: row_copy(col_of(r), col).wait_recv())
    fetches[4].wait()

    def multiply(pick, states, transposed):
        picked[...] = jnp.dot(pick[...], states[...], preferred_element_type=F32)
        for first in range(0, slots, 4):
            part = picked[first * nvec:(first + 4) * nvec].astype(BF16)
            none = jnp.zeros((2 * nvec, width), BF16)
            left = jnp.concatenate(
                [
                    jnp.concatenate([part[:2 * nvec], none], axis=1),
                    jnp.concatenate([none, part[2 * nvec:]], axis=1),
                ],
                axis=0,
            )
            b0, b1, b2, b3 = (held[first + index] for index in range(4))
            if transposed:
                right = jnp.concatenate(
                    [jnp.concatenate([b0, b1], axis=1), jnp.concatenate([b2, b3], axis=1)], axis=0
                )
                dims = (((1,), (0,)), ((), ()))
            else:
                right = jnp.concatenate(
                    [jnp.concatenate([b0, b2], axis=1), jnp.concatenate([b1, b3], axis=1)], axis=0
                )
                dims = (((1,), (1,)), ((), ()))
            both = lax.dot_general(left, right, dims, preferred_element_type=F32)
            for index in range(4):
                lanes = slice(index % 2 * width, (index % 2 + 1) * width)
                start = (first + index) * nvec
                terms[start:start + nvec] = both[index * nvec:(index + 1) * nvec, lanes]

    multiply(row_pick, row_st, True)
    low[...] = split_dot(col_place[...], terms[...])
    half = n_chip * piece
    theirs = pl.ds(pl.multiple_of((1 - core) * half, half), half)
    ours = pl.ds(pl.multiple_of(core * half, half), half)
    swap = pltpu.make_async_remote_copy(
        low.at[theirs], low_sib, sib_send.at[0], sib_recv.at[0], device_id=sibling, device_id_type=MESH
    )

    @pl.when(core == 1)
    def _():
        pl.semaphore_wait(sib_ready, 1)

    swap.start()
    swap.wait_recv()
    low_sib[...] += low[ours]

    def low_copy(source, target):
        return pltpu.make_async_remote_copy(
            low_sib.at[pieces(target)], low_in.at[pieces(source)], low_send.at[target], low_recv.at[source],
            device_id={"row": target * 2 + core, "col": col}, device_id_type=MESH,
        )

    def pass_low(q):
        col_copy(q, chip).wait_recv()
        low_copy(chip, q).start()

    loop(chip + 1, n_chip, pass_low)
    relay = pltpu.make_async_remote_copy(
        col_st.at[ours], col_st.at[ours], sib_send.at[1], sib_recv.at[1], device_id=sibling, device_id_type=MESH
    )
    relay.start()
    relay.wait_recv()

    multiply(col_pick, col_st, False)
    up[...] = split_dot(row_place[...], terms[...])

    def far_first(index):
        return (col + n_y + index // 2 * (2 * (index % 2) - 1)) % n_col

    def up_copy(source, target):
        return pltpu.make_async_remote_copy(
            up.at[pieces(target)], up_in.at[pieces(source)], up_send.at[target], up_recv.at[source],
            device_id={"row": row, "col": target}, device_id_type=MESH,
        )

    loop(1, n_col, lambda index: up_copy(col, far_first(index)).start())

    def add_low(source, total):
        low_copy(source, chip).wait_recv()
        return total + low_in[pieces(source)]

    def add_up(index, total):
        source = (col + index) % n_col
        up_copy(source, col).wait_recv()
        return total + up_in[pieces(source)]

    total = low_sib[pieces(chip)] + up[pieces(col)]
    total = lax.fori_loop(0, chip, add_low, total)
    total = lax.fori_loop(1, n_col, add_up, total)
    out[:, :width] = total[:nvec]
    out[:, width:] = total[nvec:]

    loop(1, n_col, lambda index: row_copy(col, (col + index) % n_col).wait_send())
    loop(0, chip, lambda q: col_copy(chip, q).wait_send())
    swap.wait_send()
    relay.wait_send()
    loop(chip + 1, n_chip, lambda q: low_copy(chip, q).wait_send())
    loop(1, n_col, lambda index: up_copy(col, (col + index) % n_col).wait_send())


def solution(mesh):
    n_row, n_col = mesh.shape["row"], mesh.shape["col"]
    n_chip = n_row // 2

    def local(vectors, blocks, row_index, col_index, live):
        nvec, piece_width = vectors.shape
        slots, width = blocks.shape[2], blocks.shape[4]
        rows, row_count, col_count = slots * nvec, 2 * n_col * nvec, 2 * n_row * nvec
        dma = lambda n: pltpu.SemaphoreType.DMA((n,))
        return pl.pallas_call(
            functools.partial(kernel, n_chip, n_col),
            out_shape=jax.ShapeDtypeStruct((nvec, piece_width), F32),
            in_specs=[pl.BlockSpec(memory_space=pltpu.MemorySpace.HBM)] * 5,
            out_specs=pl.BlockSpec(memory_space=pltpu.VMEM),
            scratch_shapes=[
                pltpu.VMEM(vectors.shape, BF16),
                pltpu.VMEM(row_index.shape, jnp.int32),
                pltpu.VMEM(col_index.shape, jnp.int32),
                pltpu.VMEM(live.shape, jnp.int32),
                pltpu.VMEM((slots, width, width), BF16),
                pltpu.VMEM((row_count, width), BF16),
                pltpu.VMEM((col_count, width), BF16),
                pltpu.VMEM((rows, row_count), BF16),
                pltpu.VMEM((rows, col_count), BF16),
                pltpu.VMEM((row_count, rows), BF16),
                pltpu.VMEM((col_count, rows), BF16),
                pltpu.VMEM((rows, width), F32),
                pltpu.VMEM((rows, width), F32),
                pltpu.VMEM((col_count, width), F32),
                pltpu.VMEM((col_count // 2, width), F32),
                pltpu.VMEM((col_count // 2, width), F32),
                pltpu.VMEM((row_count, width), F32),
                pltpu.VMEM((row_count, width), F32),
                dma(5),
                dma(n_col), dma(n_col), dma(n_chip), dma(n_chip), dma(n_chip), dma(n_chip), dma(n_col), dma(n_col),
                dma(2), dma(2),
                pltpu.SemaphoreType.REGULAR,
            ],
            compiler_params=pltpu.CompilerParams(
                collective_id=0, has_side_effects=True, vmem_limit_bytes=60 * 1024 * 1024
            ),
        )(vectors, blocks, row_index, col_index, live)

    return jax.shard_map(
        local,
        mesh=mesh,
        in_specs=(
            P(None, ("row", "col")),
            P("row", "col", None, None, None),
            P("row", "col", None),
            P("row", "col", None),
            P("row", "col"),
        ),
        out_specs=P(None, ("row", "col")),
        check_vma=False,
    )
```

```python
import functools

import jax
import jax.numpy as jnp
from jax import lax
from jax.experimental import pallas as pl
from jax.experimental.pallas import tpu as pltpu
from jax.sharding import PartitionSpec as P

MESH = pl.DeviceIdType.MESH
BF16 = jnp.bfloat16
F32 = jnp.float32


def iota(shape, dim):
    return lax.broadcasted_iota(jnp.int32, shape, dim)


def split_dot(one_hot, terms):
    high = terms.astype(BF16)
    low = (terms - high.astype(F32)).astype(BF16)
    return jnp.dot(one_hot, high, preferred_element_type=F32) + jnp.dot(one_hot, low, preferred_element_type=F32)


def loop(first, last, body):
    def step(index, carry):
        body(index)
        return carry

    lax.fori_loop(first, last, step, 0)


def kernel(
    n_chip, n_col, vec, blocks, row_index, col_index, live, out,
    held, row_st, col_st, row_pick, col_pick, row_place, col_place,
    picked, terms, low, low_sib, low_in, up, up_in,
    fetch_sem, row_send, row_recv, chip_send, chip_recv, up_send, up_recv, sib_send, sib_recv, sib_ready,
):
    slots, width = held.shape[0], held.shape[1]
    nvec = vec.shape[0]
    piece = 2 * nvec
    rows = slots * nvec
    n_y = n_col // 2
    row, col = lax.axis_index("row"), lax.axis_index("col")
    chip, core = row // 2, row % 2
    sibling = {"row": row + 1 - 2 * core, "col": col}

    turn = jnp.where(row == 0, 1, 0)

    def swap_y(place):
        return jnp.where(place < n_col // 2, place, n_col + 2 * (n_y // 2) - 2 - place // 2 * 2 + place % 2)

    def col_of(rank):
        return swap_y((rank + turn) % n_col)

    rank = (swap_y(col) + n_col - turn) % n_col

    fetch = pltpu.make_async_copy(blocks.at[0, 0], held, fetch_sem)

    def pieces(slot):
        return pl.ds(pl.multiple_of(slot * piece, piece), piece)

    col_st[...] = jnp.zeros_like(col_st)
    mine = core * n_chip + chip

    barrier = pltpu.get_barrier_semaphore()

    def greet(device):
        pl.semaphore_signal(barrier, inc=1, device_id=device, device_id_type=MESH)

    near = jnp.minimum(chip + 7, n_chip)
    loop(chip + 1, near, lambda q: greet({"row": q * 2 + core, "col": col}))
    loop(rank + 1, n_col, lambda r: greet({"row": row, "col": col_of(r)}))
    loop(near, n_chip, lambda q: greet({"row": q * 2 + core, "col": col}))

    @pl.when(core == 1)
    def _():
        greet(sibling)

    own = vec[...].astype(F32)
    own = jnp.concatenate([own[:, :width], own[:, width:]], axis=0).astype(BF16)
    col_st[pieces(mine)] = own
    row_st[pieces(col)] = own

    earlier = rank + chip + 1 - core

    @pl.when(earlier > 0)
    def _():
        pl.semaphore_wait(barrier, earlier)

    @pl.when(core == 0)
    def _():
        pl.semaphore_signal(sib_ready, inc=1, device_id=sibling, device_id_type=MESH)

    def col_copy(source, target):
        place = pieces(core * n_chip + source)
        return pltpu.make_async_remote_copy(
            col_st.at[place], col_st.at[place], chip_send.at[target], chip_recv.at[source],
            device_id={"row": target * 2 + core, "col": col}, device_id_type=MESH,
        )

    def row_copy(source, target):
        return pltpu.make_async_remote_copy(
            row_st.at[pieces(source)], row_st.at[pieces(source)], row_send, row_recv.at[source],
            device_id={"row": row, "col": target}, device_id_type=MESH,
        )

    loop(0, chip, lambda q: col_copy(chip, q).start())
    loop(0, rank, lambda r: row_copy(col, col_of(r)).start())
    fetch.start()

    alive = iota((1, slots), 1) < live[0, 0]
    row_ids = jnp.where(alive, row_index[0], -1).astype(F32)
    col_ids = jnp.where(alive, col_index[0], -1).astype(F32)
    spread = (iota((slots, rows), 1) // nvec == iota((slots, rows), 0)).astype(F32).astype(BF16)
    spread_t = (iota((rows, slots), 0) // nvec == iota((rows, slots), 1)).astype(F32)

    def row_target(ids, vector):
        return jnp.where(ids < 0, -1, ids * nvec + vector)

    def col_target(ids, vector):
        place = (ids // 2) % 2 * n_chip + ids // 4
        return jnp.where(ids < 0, -1, place * piece + ids % 2 * nvec + vector)

    for ids, target, pick, place in (
        (row_ids, row_target, row_pick, row_place),
        (col_ids, col_target, col_pick, col_place),
    ):
        count = place.shape[0]
        lane = jnp.dot(ids.astype(BF16), spread, preferred_element_type=F32).astype(jnp.int32)
        lane = target(lane, iota((1, rows), 1) % nvec)
        place[...] = (iota((count, rows), 0) == lane).astype(F32).astype(BF16)
        line = jnp.sum(spread_t * ids, axis=1, keepdims=True).astype(jnp.int32)
        line = target(line, iota((rows, 1), 0) % nvec)
        pick[...] = (iota((rows, count), 1) == line).astype(F32).astype(BF16)

    def answer(r):
        other = col_of(r)
        row_copy(other, col).wait_recv()
        row_copy(col, other).start()

    loop(rank + 1, n_col, answer)
    loop(0, rank, lambda r: row_copy(col_of(r), col).wait_recv())
    fetch.wait()

    def multiply(pick, states, transposed):
        picked[...] = jnp.dot(pick[...], states[...], preferred_element_type=F32)
        for first in range(0, slots, 4):
            part = picked[first * nvec:(first + 4) * nvec].astype(BF16)
            none = jnp.zeros((2 * nvec, width), BF16)
            left = jnp.concatenate(
                [
                    jnp.concatenate([part[:2 * nvec], none], axis=1),
                    jnp.concatenate([none, part[2 * nvec:]], axis=1),
                ],
                axis=0,
            )
            b0, b1, b2, b3 = (held[first + index] for index in range(4))
            if transposed:
                right = jnp.concatenate(
                    [jnp.concatenate([b0, b1], axis=1), jnp.concatenate([b2, b3], axis=1)], axis=0
                )
                dims = (((1,), (0,)), ((), ()))
            else:
                right = jnp.concatenate(
                    [jnp.concatenate([b0, b2], axis=1), jnp.concatenate([b1, b3], axis=1)], axis=0
                )
                dims = (((1,), (1,)), ((), ()))
            both = lax.dot_general(left, right, dims, preferred_element_type=F32)
            for index in range(4):
                lanes = slice(index % 2 * width, (index % 2 + 1) * width)
                start = (first + index) * nvec
                terms[start:start + nvec] = both[index * nvec:(index + 1) * nvec, lanes]

    multiply(row_pick, row_st, True)
    low[...] = split_dot(col_place[...], terms[...])
    half = n_chip * piece
    theirs = pl.ds(pl.multiple_of((1 - core) * half, half), half)
    ours = pl.ds(pl.multiple_of(core * half, half), half)
    swap = pltpu.make_async_remote_copy(
        low.at[theirs], low_sib, sib_send.at[0], sib_recv.at[0], device_id=sibling, device_id_type=MESH
    )

    @pl.when(core == 1)
    def _():
        pl.semaphore_wait(sib_ready, 1)

    swap.start()
    swap.wait_recv()
    low_sib[...] += low[ours]

    def low_copy(source, target):
        return pltpu.make_async_remote_copy(
            low_sib.at[pieces(target)], low_in.at[pieces(source)], chip_send.at[target], chip_recv.at[source],
            device_id={"row": target * 2 + core, "col": col}, device_id_type=MESH,
        )

    def pass_low(q):
        col_copy(q, chip).wait_recv()
        low_copy(chip, q).start()

    late = n_chip // 2
    first_late = jnp.maximum(chip + 1, late)
    loop(chip + 1, late, pass_low)
    loop(first_late, n_chip, lambda q: col_copy(q, chip).wait_recv())
    relay = pltpu.make_async_remote_copy(
        col_st.at[ours], col_st.at[ours], sib_send.at[1], sib_recv.at[1], device_id=sibling, device_id_type=MESH
    )
    relay.start()
    loop(first_late, n_chip, lambda q: low_copy(chip, q).start())
    relay.wait_recv()

    multiply(col_pick, col_st, False)
    up[...] = split_dot(row_place[...], terms[...])

    def up_copy(source, target):
        return pltpu.make_async_remote_copy(
            up.at[pieces(target)], up_in.at[pieces(source)], up_send, up_recv,
            device_id={"row": row, "col": target}, device_id_type=MESH,
        )

    loop(0, rank, lambda r: up_copy(col, col_of(r)).start())
    loop(rank + 1, n_col, lambda r: up_copy(col, col_of(r)).start())

    def add_low(source, total):
        low_copy(source, chip).wait_recv()
        return total + low_in[pieces(source)]

    def add_up(index, total):
        return total + up_in[pieces((col + index) % n_col)]

    total = low_sib[pieces(chip)] + up[pieces(col)]
    total = lax.fori_loop(0, chip, add_low, total)
    every_up = up_in.at[pl.ds(0, (n_col - 1) * piece)]
    every_up = pltpu.make_async_remote_copy(
        every_up, every_up, up_send, up_recv, device_id=sibling, device_id_type=MESH
    )
    every_up.wait_recv()
    total = lax.fori_loop(1, n_col, add_up, total)
    out[:, :width] = total[:nvec]
    out[:, width:] = total[nvec:]

    every_row = row_st.at[pl.ds(0, (n_col - 1) * piece)]
    pltpu.make_async_remote_copy(
        every_row, every_row, row_send, row_send, device_id=sibling, device_id_type=MESH
    ).wait_send()
    loop(0, chip, lambda q: col_copy(chip, q).wait_send())
    swap.wait_send()
    relay.wait_send()
    loop(chip + 1, n_chip, lambda q: low_copy(chip, q).wait_send())
    every_up.wait_send()


def solution(mesh):
    n_row, n_col = mesh.shape["row"], mesh.shape["col"]
    n_chip = n_row // 2

    def local(vectors, blocks, row_index, col_index, live):
        nvec, piece_width = vectors.shape
        slots, width = blocks.shape[2], blocks.shape[4]
        rows, row_count, col_count = slots * nvec, 2 * n_col * nvec, 2 * n_row * nvec
        vmem, smem = pl.BlockSpec(memory_space=pltpu.VMEM), pl.BlockSpec(memory_space=pltpu.SMEM)
        one = pltpu.SemaphoreType.DMA
        dma = lambda n: pltpu.SemaphoreType.DMA((n,))
        return pl.pallas_call(
            functools.partial(kernel, n_chip, n_col),
            out_shape=jax.ShapeDtypeStruct((nvec, piece_width), F32),
            in_specs=[vmem, pl.BlockSpec(memory_space=pltpu.MemorySpace.HBM), vmem, vmem, smem],
            out_specs=vmem,
            scratch_shapes=[
                pltpu.VMEM((slots, width, width), BF16),
                pltpu.VMEM((row_count, width), BF16),
                pltpu.VMEM((col_count, width), BF16),
                pltpu.VMEM((rows, row_count), BF16),
                pltpu.VMEM((rows, col_count), BF16),
                pltpu.VMEM((row_count, rows), BF16),
                pltpu.VMEM((col_count, rows), BF16),
                pltpu.VMEM((rows, width), F32),
                pltpu.VMEM((rows, width), F32),
                pltpu.VMEM((col_count, width), F32),
                pltpu.VMEM((col_count // 2, width), F32),
                pltpu.VMEM((col_count // 2, width), F32),
                pltpu.VMEM((row_count, width), F32),
                pltpu.VMEM((row_count, width), F32),
                one,
                one, dma(n_col), dma(n_chip), dma(n_chip), one, one, dma(2), dma(2),
                pltpu.SemaphoreType.REGULAR,
            ],
            compiler_params=pltpu.CompilerParams(
                collective_id=0, has_side_effects=True, vmem_limit_bytes=53 * 1024 * 1024
            ),
        )(vectors, blocks, row_index, col_index, live)

    return jax.shard_map(
        local,
        mesh=mesh,
        in_specs=(
            P(None, ("row", "col")),
            P("row", "col", None, None, None),
            P("row", "col", None),
            P("row", "col", None),
            P("row", "col"),
        ),
        out_specs=P(None, ("row", "col")),
        check_vma=False,
    )
```

```python
import functools

import jax
import jax.numpy as jnp
from jax import lax
from jax.experimental import pallas as pl
from jax.experimental.pallas import tpu as pltpu
from jax.sharding import PartitionSpec as P

MESH = pl.DeviceIdType.MESH
BF16 = jnp.bfloat16
F32 = jnp.float32


def iota(shape, dim):
    return lax.broadcasted_iota(jnp.int32, shape, dim)


def split_dot(one_hot, terms):
    high = terms.astype(BF16)
    low = (terms - high.astype(F32)).astype(BF16)
    return jnp.dot(one_hot, high, preferred_element_type=F32) + jnp.dot(one_hot, low, preferred_element_type=F32)


def loop(first, last, body):
    def step(index, carry):
        body(index)
        return carry

    lax.fori_loop(first, last, step, 0)


def kernel(
    n_chip, n_col, vec, blocks, row_index, col_index, live, out,
    held, row_st, col_st, row_pick, col_pick, row_place, col_place,
    picked, terms, low, low_sib, low_in, up, up_in,
    fetch_sem, row_send, row_recv, chip_send, chip_recv, up_send, up_recv, cross_send, cross_recv, sib_send, sib_recv, sib_ready,
):
    slots, width = held.shape[0], held.shape[1]
    nvec = vec.shape[0]
    piece = 2 * nvec
    rows = slots * nvec
    n_y = n_col // 2
    row, col = lax.axis_index("row"), lax.axis_index("col")
    chip, core = row // 2, row % 2
    sibling = {"row": row + 1 - 2 * core, "col": col}

    turn = jnp.where(row == 0, 1, 0)

    def swap_y(place):
        return jnp.where(place < n_col // 2, place, n_col + 2 * (n_y // 2) - 2 - place // 2 * 2 + place % 2)

    def col_of(rank):
        return swap_y((rank + turn) % n_col)

    rank = (swap_y(col) + n_col - turn) % n_col

    fetch = pltpu.make_async_copy(blocks.at[0, 0], held, fetch_sem)

    def pieces(slot):
        return pl.ds(pl.multiple_of(slot * piece, piece), piece)

    col_st[...] = jnp.zeros_like(col_st)
    late = n_chip // 2

    def spot(owner, source):
        return source // late * n_chip + owner * late + source % late

    mine = spot(core, chip)

    barrier = pltpu.get_barrier_semaphore()

    def greet(device):
        pl.semaphore_signal(barrier, inc=1, device_id=device, device_id_type=MESH)

    near = jnp.minimum(chip + 7, n_chip)
    loop(chip + 1, near, lambda q: greet({"row": q * 2 + core, "col": col}))
    loop(rank + 1, n_col, lambda r: greet({"row": row, "col": col_of(r)}))
    loop(near, n_chip, lambda q: greet({"row": q * 2 + core, "col": col}))

    hurried = chip == 0

    @pl.when(hurried)
    def _():
        loop(late, n_chip, lambda q: greet({"row": q * 2 + 1 - core, "col": col}))

    @pl.when(core == 1)
    def _():
        greet(sibling)

    own = vec[...].astype(F32)
    own = jnp.concatenate([own[:, :width], own[:, width:]], axis=0).astype(BF16)
    col_st[pieces(mine)] = own
    row_st[pieces(col)] = own

    earlier = rank + chip + 1 - core + jnp.where(chip >= late, 1, 0)

    @pl.when(earlier > 0)
    def _():
        pl.semaphore_wait(barrier, earlier)

    @pl.when(core == 0)
    def _():
        pl.semaphore_signal(sib_ready, inc=1, device_id=sibling, device_id_type=MESH)

    def col_copy(source, target):
        place = pieces(spot(core, source))
        return pltpu.make_async_remote_copy(
            col_st.at[place], col_st.at[place], chip_send.at[target], chip_recv.at[source],
            device_id={"row": target * 2 + core, "col": col}, device_id_type=MESH,
        )

    def row_copy(source, target):
        return pltpu.make_async_remote_copy(
            row_st.at[pieces(source)], row_st.at[pieces(source)], row_send, row_recv.at[source],
            device_id={"row": row, "col": target}, device_id_type=MESH,
        )

    def cross_copy(place):
        return pltpu.make_async_remote_copy(
            col_st.at[place], col_st.at[place], cross_send, cross_recv,
            device_id={"row": 1 - core, "col": col}, device_id_type=MESH,
        )

    ahead = jnp.minimum(chip, 6)
    loop(0, ahead, lambda q: col_copy(chip, q).start())

    @pl.when(chip >= late)
    def _():
        cross_copy(pieces(mine)).start()

    loop(ahead, chip, lambda q: col_copy(chip, q).start())
    loop(0, rank, lambda r: row_copy(col, col_of(r)).start())
    fetch.start()

    alive = iota((1, slots), 1) < live[0, 0]
    row_ids = jnp.where(alive, row_index[0], -1).astype(F32)
    col_ids = jnp.where(alive, col_index[0], -1).astype(F32)
    spread = (iota((slots, rows), 1) // nvec == iota((slots, rows), 0)).astype(F32).astype(BF16)
    spread_t = (iota((rows, slots), 0) // nvec == iota((rows, slots), 1)).astype(F32)

    def row_target(ids, vector):
        return jnp.where(ids < 0, -1, ids * nvec + vector)

    def col_target(ids, vector):
        place = (ids // 2) % 2 * n_chip + ids // 4
        return jnp.where(ids < 0, -1, place * piece + ids % 2 * nvec + vector)

    def spot_target(ids, vector):
        place = spot((ids // 2) % 2, ids // 4)
        return jnp.where(ids < 0, -1, place * piece + ids % 2 * nvec + vector)

    for ids, target, source, pick, place in (
        (row_ids, row_target, row_target, row_pick, row_place),
        (col_ids, col_target, spot_target, col_pick, col_place),
    ):
        count = place.shape[0]
        lane = jnp.dot(ids.astype(BF16), spread, preferred_element_type=F32).astype(jnp.int32)
        lane = target(lane, iota((1, rows), 1) % nvec)
        place[...] = (iota((count, rows), 0) == lane).astype(F32).astype(BF16)
        line = jnp.sum(spread_t * ids, axis=1, keepdims=True).astype(jnp.int32)
        line = source(line, iota((rows, 1), 0) % nvec)
        pick[...] = (iota((rows, count), 1) == line).astype(F32).astype(BF16)

    def answer(r):
        other = col_of(r)
        row_copy(other, col).wait_recv()
        row_copy(col, other).start()

    loop(rank + 1, n_col, answer)
    loop(0, rank, lambda r: row_copy(col_of(r), col).wait_recv())
    fetch.wait()

    def multiply():
        for first in range(0, slots, 4):
            part = picked[first * nvec:(first + 4) * nvec].astype(BF16)
            none = jnp.zeros((2 * nvec, width), BF16)
            left = jnp.concatenate(
                [
                    jnp.concatenate([part[:2 * nvec], none], axis=1),
                    jnp.concatenate([none, part[2 * nvec:]], axis=1),
                ],
                axis=0,
            )
            b0, b1, b2, b3 = (held[first + index] for index in range(4))
            right = jnp.concatenate(
                [jnp.concatenate([b0, b1], axis=1), jnp.concatenate([b2, b3], axis=1)], axis=0
            )
            both = jnp.dot(left, right, preferred_element_type=F32)
            for index in range(4):
                lanes = slice(index % 2 * width, (index % 2 + 1) * width)
                start = (first + index) * nvec
                terms[start:start + nvec] = both[index * nvec:(index + 1) * nvec, lanes]

    picked[...] = jnp.dot(row_pick[...], row_st[...], preferred_element_type=F32)
    multiply()
    low[...] = split_dot(col_place[...], terms[...])
    half = n_chip * piece
    theirs = pl.ds(pl.multiple_of((1 - core) * half, half), half)
    ours = pl.ds(pl.multiple_of(core * half, half), half)
    swap = pltpu.make_async_remote_copy(
        low.at[theirs], low_sib, sib_send.at[0], sib_recv.at[0], device_id=sibling, device_id_type=MESH
    )

    @pl.when(core == 1)
    def _():
        pl.semaphore_wait(sib_ready, 1)

    swap.start()

    def take_low():
        swap.wait_recv()
        low_sib[...] += low[ours]

    def low_copy(source, target):
        return pltpu.make_async_remote_copy(
            low_sib.at[pieces(target)], low_in.at[pieces(source)], chip_send.at[target], chip_recv.at[source],
            device_id={"row": target * 2 + core, "col": col}, device_id_type=MESH,
        )

    def pass_low(q):
        col_copy(q, chip).wait_recv()
        low_copy(chip, q).start()

    first_late = jnp.maximum(chip + 1, late)

    @pl.when(hurried)
    def _():
        loop(chip + 1, late, lambda q: col_copy(q, chip).wait_recv())

    @pl.when(jnp.logical_not(hurried))
    def _():
        take_low()
        loop(chip + 1, late, pass_low)

    quarter = late * piece

    def relay(group):
        place = pl.ds(pl.multiple_of(group * half + core * quarter, quarter), quarter)
        return pltpu.make_async_remote_copy(
            col_st.at[place], col_st.at[place], sib_send.at[1 + group], sib_recv.at[1 + group],
            device_id=sibling, device_id_type=MESH,
        )

    @pl.when(chip < late)
    def _():
        relay(0).start()

    for slot in range(slots):
        held[slot] = held[slot].T

    @pl.when(chip < late)
    def _():
        relay(0).wait_recv()

    picked[...] = jnp.dot(col_pick[:, :half], col_st[:half], preferred_element_type=F32)
    loop(first_late, n_chip, lambda q: col_copy(q, chip).wait_recv())
    every_late = pl.ds(0, (n_chip - late) * piece)

    @pl.when(hurried)
    def _():
        cross_copy(every_late).wait_recv()

    @pl.when(jnp.logical_not(hurried))
    def _():
        relay(1).start()
        loop(first_late, n_chip, lambda q: low_copy(chip, q).start())
        relay(1).wait_recv()

    picked[...] += jnp.dot(col_pick[:, half:], col_st[half:], preferred_element_type=F32)
    multiply()
    up[...] = split_dot(row_place[...], terms[...])

    def up_copy(source, target):
        return pltpu.make_async_remote_copy(
            up.at[pieces(target)], up_in.at[pieces(source)], up_send, up_recv,
            device_id={"row": row, "col": target}, device_id_type=MESH,
        )

    loop(0, rank, lambda r: up_copy(col, col_of(r)).start())
    loop(rank + 1, n_col, lambda r: up_copy(col, col_of(r)).start())

    @pl.when(hurried)
    def _():
        take_low()
        loop(chip + 1, n_chip, lambda q: low_copy(chip, q).start())

    def add_low(source, total):
        low_copy(source, chip).wait_recv()
        return total + low_in[pieces(source)]

    def add_up(index, total):
        return total + up_in[pieces((col + index) % n_col)]

    total = low_sib[pieces(chip)] + up[pieces(col)]
    total = lax.fori_loop(0, chip, add_low, total)
    every_up = up_in.at[pl.ds(0, (n_col - 1) * piece)]
    every_up = pltpu.make_async_remote_copy(
        every_up, every_up, up_send, up_recv, device_id=sibling, device_id_type=MESH
    )
    every_up.wait_recv()
    total = lax.fori_loop(1, n_col, add_up, total)
    out[:, :width] = total[:nvec]
    out[:, width:] = total[nvec:]

    every_row = row_st.at[pl.ds(0, (n_col - 1) * piece)]
    pltpu.make_async_remote_copy(
        every_row, every_row, row_send, row_send, device_id=sibling, device_id_type=MESH
    ).wait_send()
    loop(0, chip, lambda q: col_copy(chip, q).wait_send())
    swap.wait_send()

    @pl.when(jnp.logical_not(hurried))
    def _():
        relay(1).wait_send()

    @pl.when(chip >= late)
    def _():
        cross_copy(pieces(mine)).wait_send()

    @pl.when(chip < late)
    def _():
        relay(0).wait_send()

    loop(chip + 1, n_chip, lambda q: low_copy(chip, q).wait_send())
    every_up.wait_send()


def solution(mesh):
    n_row, n_col = mesh.shape["row"], mesh.shape["col"]
    n_chip = n_row // 2

    def local(vectors, blocks, row_index, col_index, live):
        nvec, piece_width = vectors.shape
        slots, width = blocks.shape[2], blocks.shape[4]
        rows, row_count, col_count = slots * nvec, 2 * n_col * nvec, 2 * n_row * nvec
        vmem, smem = pl.BlockSpec(memory_space=pltpu.VMEM), pl.BlockSpec(memory_space=pltpu.SMEM)
        one = pltpu.SemaphoreType.DMA
        dma = lambda n: pltpu.SemaphoreType.DMA((n,))
        return pl.pallas_call(
            functools.partial(kernel, n_chip, n_col),
            out_shape=jax.ShapeDtypeStruct((nvec, piece_width), F32),
            in_specs=[vmem, pl.BlockSpec(memory_space=pltpu.MemorySpace.HBM), vmem, vmem, smem],
            out_specs=vmem,
            scratch_shapes=[
                pltpu.VMEM((slots, width, width), BF16),
                pltpu.VMEM((row_count, width), BF16),
                pltpu.VMEM((col_count, width), BF16),
                pltpu.VMEM((rows, row_count), BF16),
                pltpu.VMEM((rows, col_count), BF16),
                pltpu.VMEM((row_count, rows), BF16),
                pltpu.VMEM((col_count, rows), BF16),
                pltpu.VMEM((rows, width), F32),
                pltpu.VMEM((rows, width), F32),
                pltpu.VMEM((col_count, width), F32),
                pltpu.VMEM((col_count // 2, width), F32),
                pltpu.VMEM((col_count // 2, width), F32),
                pltpu.VMEM((row_count, width), F32),
                pltpu.VMEM((row_count, width), F32),
                one,
                one, dma(n_col), dma(n_chip), dma(n_chip), one, one, one, one, dma(3), dma(3),
                pltpu.SemaphoreType.REGULAR,
            ],
            compiler_params=pltpu.CompilerParams(
                collective_id=0, has_side_effects=True, vmem_limit_bytes=53 * 1024 * 1024
            ),
        )(vectors, blocks, row_index, col_index, live)

    return jax.shard_map(
        local,
        mesh=mesh,
        in_specs=(
            P(None, ("row", "col")),
            P("row", "col", None, None, None),
            P("row", "col", None),
            P("row", "col", None),
            P("row", "col"),
        ),
        out_specs=P(None, ("row", "col")),
        check_vma=False,
    )
```

```python
import functools

import jax
import jax.numpy as jnp
from jax import lax
from jax.experimental import pallas as pl
from jax.experimental.pallas import tpu as pltpu
from jax.sharding import PartitionSpec as P

MESH = pl.DeviceIdType.MESH
BF16 = jnp.bfloat16
F32 = jnp.float32


def iota(shape, dim):
    return lax.broadcasted_iota(jnp.int32, shape, dim)


def split_dot(one_hot, terms):
    high = terms.astype(BF16)
    low = (terms - high.astype(F32)).astype(BF16)
    return jnp.dot(one_hot, high, preferred_element_type=F32) + jnp.dot(one_hot, low, preferred_element_type=F32)


def loop(first, last, body):
    def step(index, carry):
        body(index)
        return carry

    lax.fori_loop(first, last, step, 0)


def kernel(
    n_chip, n_col, vec, blocks, row_index, col_index, live, out,
    held, row_st, col_st, row_pick, col_pick, row_place, col_place,
    picked, terms, low, low_sib, low_in, up, up_in,
    fetch_sem, row_send, row_recv, chip_send, chip_recv, up_send, up_recv, cross_send, cross_recv, sib_send, sib_recv, sib_ready,
):
    slots, width = held.shape[0], held.shape[1]
    nvec = vec.shape[0]
    piece = 2 * nvec
    rows = slots * nvec
    n_y = n_col // 2
    row, col = lax.axis_index("row"), lax.axis_index("col")
    chip, core = row // 2, row % 2
    sibling = {"row": row + 1 - 2 * core, "col": col}

    turn = jnp.where(row == 0, 1, 0)

    def swap_y(place):
        return jnp.where(place < n_col // 2, place, n_col + 2 * (n_y // 2) - 2 - place // 2 * 2 + place % 2)

    def col_of(rank):
        return swap_y((rank + turn) % n_col)

    rank = (swap_y(col) + n_col - turn) % n_col

    fetch = pltpu.make_async_copy(blocks.at[0, 0], held, fetch_sem)

    def pieces(slot):
        return pl.ds(pl.multiple_of(slot * piece, piece), piece)

    col_st[...] = jnp.zeros_like(col_st)
    late = n_chip // 2

    def spot(owner, source):
        return source // late * n_chip + owner * late + source % late

    mine = spot(core, chip)

    barrier = pltpu.get_barrier_semaphore()

    def greet(device):
        pl.semaphore_signal(barrier, inc=1, device_id=device, device_id_type=MESH)

    near = jnp.minimum(chip + 7, n_chip)
    loop(chip + 1, near, lambda q: greet({"row": q * 2 + core, "col": col}))
    loop(rank + 1, n_col, lambda r: greet({"row": row, "col": col_of(r)}))
    loop(near, n_chip, lambda q: greet({"row": q * 2 + core, "col": col}))

    hurried = chip == 0

    @pl.when(hurried)
    def _():
        loop(late, n_chip, lambda q: greet({"row": q * 2 + 1 - core, "col": col}))

    @pl.when(core == 1)
    def _():
        greet(sibling)

    own = vec[...].astype(F32)
    own = jnp.concatenate([own[:, :width], own[:, width:]], axis=0).astype(BF16)
    col_st[pieces(mine)] = own
    row_st[pieces(col)] = own

    earlier = rank + chip + 1 - core + jnp.where(chip >= late, 1, 0)

    @pl.when(earlier > 0)
    def _():
        pl.semaphore_wait(barrier, earlier)

    @pl.when(core == 0)
    def _():
        pl.semaphore_signal(sib_ready, inc=1, device_id=sibling, device_id_type=MESH)

    def col_copy(source, target):
        place = pieces(spot(core, source))
        return pltpu.make_async_remote_copy(
            col_st.at[place], col_st.at[place], chip_send.at[target], chip_recv.at[source],
            device_id={"row": target * 2 + core, "col": col}, device_id_type=MESH,
        )

    def row_copy(source, target):
        return pltpu.make_async_remote_copy(
            row_st.at[pieces(source)], row_st.at[pieces(source)], row_send, row_recv.at[source],
            device_id={"row": row, "col": target}, device_id_type=MESH,
        )

    def cross_copy(place):
        return pltpu.make_async_remote_copy(
            col_st.at[place], col_st.at[place], cross_send, cross_recv,
            device_id={"row": 1 - core, "col": col}, device_id_type=MESH,
        )

    ahead = jnp.minimum(chip, 6)
    loop(0, ahead, lambda q: col_copy(chip, q).start())

    @pl.when(chip >= late)
    def _():
        cross_copy(pieces(mine)).start()

    loop(ahead, chip, lambda q: col_copy(chip, q).start())
    loop(0, rank, lambda r: row_copy(col, col_of(r)).start())
    fetch.start()

    alive = iota((1, slots), 1) < live[0, 0]
    row_ids = jnp.where(alive, row_index[0], -1).astype(F32)
    col_ids = jnp.where(alive, col_index[0], -1).astype(F32)
    spread = (iota((slots, rows), 1) // nvec == iota((slots, rows), 0)).astype(F32).astype(BF16)
    spread_t = (iota((rows, slots), 0) // nvec == iota((rows, slots), 1)).astype(F32)

    def row_target(ids, vector):
        return jnp.where(ids < 0, -1, ids * nvec + vector)

    def col_target(ids, vector):
        place = (ids // 2) % 2 * n_chip + ids // 4
        return jnp.where(ids < 0, -1, place * piece + ids % 2 * nvec + vector)

    def spot_target(ids, vector):
        place = spot((ids // 2) % 2, ids // 4)
        return jnp.where(ids < 0, -1, place * piece + ids % 2 * nvec + vector)

    for ids, target, source, pick, place in (
        (row_ids, row_target, row_target, row_pick, row_place),
        (col_ids, col_target, spot_target, col_pick, col_place),
    ):
        count = place.shape[0]
        lane = jnp.dot(ids.astype(BF16), spread, preferred_element_type=F32).astype(jnp.int32)
        lane = target(lane, iota((1, rows), 1) % nvec)
        place[...] = (iota((count, rows), 0) == lane).astype(F32).astype(BF16)
        line = jnp.sum(spread_t * ids, axis=1, keepdims=True).astype(jnp.int32)
        line = source(line, iota((rows, 1), 0) % nvec)
        pick[...] = (iota((rows, count), 1) == line).astype(F32).astype(BF16)

    def answer(r):
        other = col_of(r)
        row_copy(other, col).wait_recv()
        row_copy(col, other).start()

    loop(rank + 1, n_col, answer)
    loop(0, rank, lambda r: row_copy(col_of(r), col).wait_recv())
    fetch.wait()

    def multiply():
        for first in range(0, slots, 4):
            part = picked[first * nvec:(first + 4) * nvec].astype(BF16)
            none = jnp.zeros((2 * nvec, width), BF16)
            left = jnp.concatenate(
                [
                    jnp.concatenate([part[:2 * nvec], none], axis=1),
                    jnp.concatenate([none, part[2 * nvec:]], axis=1),
                ],
                axis=0,
            )
            b0, b1, b2, b3 = (held[first + index] for index in range(4))
            right = jnp.concatenate(
                [jnp.concatenate([b0, b1], axis=1), jnp.concatenate([b2, b3], axis=1)], axis=0
            )
            both = jnp.dot(left, right, preferred_element_type=F32)
            for index in range(4):
                lanes = slice(index % 2 * width, (index % 2 + 1) * width)
                start = (first + index) * nvec
                terms[start:start + nvec] = both[index * nvec:(index + 1) * nvec, lanes]

    picked[...] = jnp.dot(row_pick[...], row_st[...], preferred_element_type=F32)
    multiply()
    low[...] = split_dot(col_place[...], terms[...])
    half = n_chip * piece
    theirs = pl.ds(pl.multiple_of((1 - core) * half, half), half)
    ours = pl.ds(pl.multiple_of(core * half, half), half)
    swap = pltpu.make_async_remote_copy(
        low.at[theirs], low_sib, sib_send.at[0], sib_recv.at[0], device_id=sibling, device_id_type=MESH
    )

    @pl.when(core == 1)
    def _():
        pl.semaphore_wait(sib_ready, 1)

    swap.start()

    def take_low():
        swap.wait_recv()
        low_sib[...] += low[ours]

    def low_copy(source, target):
        return pltpu.make_async_remote_copy(
            low_sib.at[pieces(target)], low_in.at[pieces(source)], chip_send.at[target], chip_recv.at[source],
            device_id={"row": target * 2 + core, "col": col}, device_id_type=MESH,
        )

    def pass_low(q):
        col_copy(q, chip).wait_recv()
        low_copy(chip, q).start()

    first_late = jnp.maximum(chip + 1, late)

    @pl.when(hurried)
    def _():
        loop(chip + 1, late, lambda q: col_copy(q, chip).wait_recv())

    @pl.when(jnp.logical_not(hurried))
    def _():
        take_low()
        loop(chip + 1, late, pass_low)

    quarter = late * piece

    def relay(group):
        place = pl.ds(pl.multiple_of(group * half + core * quarter, quarter), quarter)
        return pltpu.make_async_remote_copy(
            col_st.at[place], col_st.at[place], sib_send.at[1 + group], sib_recv.at[1 + group],
            device_id=sibling, device_id_type=MESH,
        )

    @pl.when(chip < late)
    def _():
        relay(0).start()

    for slot in range(slots):
        held[slot] = held[slot].T

    @pl.when(chip < late)
    def _():
        relay(0).wait_recv()

    picked[...] = jnp.dot(col_pick[:, :half], col_st[:half], preferred_element_type=F32)
    loop(first_late, n_chip, lambda q: col_copy(q, chip).wait_recv())
    every_late = pl.ds(0, (n_chip - late) * piece)

    @pl.when(hurried)
    def _():
        cross_copy(every_late).wait_recv()

    @pl.when(jnp.logical_not(hurried))
    def _():
        relay(1).start()
        loop(first_late, n_chip, lambda q: low_copy(chip, q).start())
        relay(1).wait_recv()

    picked[...] += jnp.dot(col_pick[:, half:], col_st[half:], preferred_element_type=F32)
    multiply()
    up[...] = split_dot(row_place[...], terms[...])

    def up_copy(source, target):
        return pltpu.make_async_remote_copy(
            up.at[pieces(target)], up_in.at[pieces(source)], up_send, up_recv,
            device_id={"row": row, "col": target}, device_id_type=MESH,
        )

    loop(0, rank, lambda r: up_copy(col, col_of(r)).start())
    loop(rank + 1, n_col, lambda r: up_copy(col, col_of(r)).start())

    @pl.when(hurried)
    def _():
        take_low()
        loop(chip + 1, n_chip, lambda q: low_copy(chip, q).start())

    def add_low(source, total):
        low_copy(source, chip).wait_recv()
        return total + low_in[pieces(source)]

    up_in[pieces(col)] = up[pieces(col)]
    total = low_sib[pieces(chip)]
    total = lax.fori_loop(0, chip, add_low, total)
    every_up = up_in.at[pl.ds(0, (n_col - 1) * piece)]
    every_up = pltpu.make_async_remote_copy(
        every_up, every_up, up_send, up_recv, device_id=sibling, device_id_type=MESH
    )
    every_row = row_st.at[pl.ds(0, (n_col - 1) * piece)]
    pltpu.make_async_remote_copy(
        every_row, every_row, row_send, row_send, device_id=sibling, device_id_type=MESH
    ).wait_send()
    loop(0, chip, lambda q: col_copy(chip, q).wait_send())
    swap.wait_send()

    @pl.when(jnp.logical_not(hurried))
    def _():
        relay(1).wait_send()

    @pl.when(chip >= late)
    def _():
        cross_copy(pieces(mine)).wait_send()

    @pl.when(chip < late)
    def _():
        relay(0).wait_send()

    loop(chip + 1, n_chip, lambda q: low_copy(chip, q).wait_send())
    every_up.wait_recv()
    for source in range(n_col):
        total = total + up_in[source * piece:(source + 1) * piece]
    out[:, :width] = total[:nvec]
    out[:, width:] = total[nvec:]
    every_up.wait_send()


def solution(mesh):
    n_row, n_col = mesh.shape["row"], mesh.shape["col"]
    n_chip = n_row // 2

    def local(vectors, blocks, row_index, col_index, live):
        nvec, piece_width = vectors.shape
        slots, width = blocks.shape[2], blocks.shape[4]
        rows, row_count, col_count = slots * nvec, 2 * n_col * nvec, 2 * n_row * nvec
        vmem, smem = pl.BlockSpec(memory_space=pltpu.VMEM), pl.BlockSpec(memory_space=pltpu.SMEM)
        one = pltpu.SemaphoreType.DMA
        dma = lambda n: pltpu.SemaphoreType.DMA((n,))
        return pl.pallas_call(
            functools.partial(kernel, n_chip, n_col),
            out_shape=jax.ShapeDtypeStruct((nvec, piece_width), F32),
            in_specs=[vmem, pl.BlockSpec(memory_space=pltpu.MemorySpace.HBM), vmem, vmem, smem],
            out_specs=vmem,
            scratch_shapes=[
                pltpu.VMEM((slots, width, width), BF16),
                pltpu.VMEM((row_count, width), BF16),
                pltpu.VMEM((col_count, width), BF16),
                pltpu.VMEM((rows, row_count), BF16),
                pltpu.VMEM((rows, col_count), BF16),
                pltpu.VMEM((row_count, rows), BF16),
                pltpu.VMEM((col_count, rows), BF16),
                pltpu.VMEM((rows, width), F32),
                pltpu.VMEM((rows, width), F32),
                pltpu.VMEM((col_count, width), F32),
                pltpu.VMEM((col_count // 2, width), F32),
                pltpu.VMEM((col_count // 2, width), F32),
                pltpu.VMEM((row_count, width), F32),
                pltpu.VMEM((row_count, width), F32),
                one,
                one, dma(n_col), dma(n_chip), dma(n_chip), one, one, one, one, dma(3), dma(3),
                pltpu.SemaphoreType.REGULAR,
            ],
            compiler_params=pltpu.CompilerParams(
                collective_id=0, has_side_effects=True, vmem_limit_bytes=53 * 1024 * 1024
            ),
        )(vectors, blocks, row_index, col_index, live)

    return jax.shard_map(
        local,
        mesh=mesh,
        in_specs=(
            P(None, ("row", "col")),
            P("row", "col", None, None, None),
            P("row", "col", None),
            P("row", "col", None),
            P("row", "col"),
        ),
        out_specs=P(None, ("row", "col")),
        check_vma=False,
    )
```
